512 devices in a mesh: gy: 16 (over y, x), gz: 32 (over z, core).
Axes of the slice: x: 4, y: 4, z: 16, core: 2. Of those that a mesh axis runs over, the one named last changes fastest.
Arguments:
- field: float32 [256, 128, 11, 512], P('gy', 'gz'), as said below
- start_x: float32 [512, 60], replicated, may hold values from -6 to 6
- start_y: float32 [256, 60], replicated, may hold values from -6 to 6
Outputs:
- factor_x: float32 [512, 60], replicated
- factor_y: float32 [256, 60], P('gy')
- core: float32 [60, 128, 660], P(None, 'gz')
The draws below stay inside these ranges and needn't reach their ends.
Inputs may be any that keep to these rules, and one draw needn't show every extreme that they name: `field`: every entry is a real value; rows and columns carry varying scales.
All inputs are finite; a program needn't handle non-finite values.
Results may differ from the reference program's by a relative error of at most 0.0003.
Values sent between devices are 32-bit elements; how exact they have to be, the bound alone decides.
No kernel may reach another device: no remote copies, remote signals or barrier semaphores. Data moves between devices by JAX's collectives and lax.ppermute only.
A program may use at most 64 MiB of HBM per device.

```python
import jax
import jax.numpy as jnp
from jax import lax

NX = 512
V = 11
RANK = 60
ITERS = 4
NY = 256
NZ = 128


def spread_scales(key, count, top):
    level = jax.random.uniform(key, (count,), jnp.float32, -0.5, 0.5)
    return jnp.exp(level * jnp.log(jnp.float32(top)))


def draw_field(key, part):
    key = jax.random.fold_in(key, 11)
    keys = jax.random.split(key, 5)
    scale_y = spread_scales(keys[0], NY, 5.0)
    scale_z = spread_scales(keys[1], NZ, 10.0)
    scale_v = spread_scales(keys[2], V, 10.0)
    scale_x = spread_scales(keys[3], NX, 5.0)
    base = jax.random.normal(keys[4], (NY, NZ, V, NX), jnp.float32)
    return base * scale_y[:, None, None, None] * scale_z[None, :, None, None] * scale_v[None, None, :, None] * scale_x[None, None, None, :]


def noise(own_key, shape, deviation, limit, kind=jnp.bfloat16):
    return jnp.clip(deviation * jax.random.normal(own_key, shape, jnp.float32), -limit, limit).astype(kind)


def setup_inputs(seed: int = 0) -> dict:
    key_of = jax.random.split(jax.random.key(seed), 4)
    field = draw_field(jax.random.fold_in(key_of[3], 71), 0)
    start_x = noise(key_of[1], (NX, RANK), 1.0, 6.0, jnp.float32)
    start_y = noise(key_of[2], (NY, RANK), 1.0, 6.0, jnp.float32)
    return dict(field=field, start_x=start_x, start_y=start_y)


def product(left, right):
    return jnp.dot(left.astype(jnp.float32), right.astype(jnp.float32), precision=lax.Precision.HIGHEST, preferred_element_type=jnp.float32)

def orthonormal(matrix):
    small = product(matrix.T, matrix)
    lower = jnp.linalg.cholesky(small)
    return lax.linalg.triangular_solve(lower, matrix, left_side=False, lower=True, transpose_a=True)

def reference(field, start_x, start_y):
    columns = NY * NZ * V
    flat = field.reshape(columns, NX)
    gram_x = product(flat.T, flat) / columns
    factor_x = start_x
    for step in range(ITERS):
        factor_x = orthonormal(product(gram_x, factor_x))
    reduced = product(flat, factor_x).reshape(NY, NZ * V * RANK)
    gram_y = product(reduced, reduced.T) / (NZ * V * RANK)
    factor_y = start_y
    for step in range(ITERS):
        factor_y = orthonormal(product(gram_y, factor_y))
    core = product(factor_y.T, reduced) / jnp.sqrt(jnp.float32(NX * NY))
    return (factor_x, factor_y, core.reshape(RANK, NZ, V * RANK))
```

```python
import functools

import jax
import jax.numpy as jnp
from jax import lax
from jax.experimental import pallas as pl
from jax.experimental.pallas import tpu as pltpu
from jax.sharding import PartitionSpec as P

ITERS = 4
PAD = 64


def product(left, right):
    return jnp.dot(left, right, precision=lax.Precision.HIGHEST, preferred_element_type=jnp.float32)


def split(value):
    high = value.astype(jnp.bfloat16)
    rest = value - high.astype(jnp.float32)
    middle = rest.astype(jnp.bfloat16)
    low = (rest - middle.astype(jnp.float32)).astype(jnp.bfloat16)
    return high, middle, low


def matmul(left, right):
    return lax.dot_general(left, right, (((1,), (0,)), ((), ())), preferred_element_type=jnp.float32)


def matmul_t(left, right):
    return lax.dot_general(left, right, (((1,), (1,)), ((), ())), preferred_element_type=jnp.float32)


def inverse_factor(small, rank):
    rows = lax.broadcasted_iota(jnp.int32, (PAD, 2 * PAD), 0)
    lanes = lax.broadcasted_iota(jnp.int32, (PAD, 2 * PAD), 1)
    unit = jnp.where(lanes == rows + PAD, 1.0, 0.0)
    both = jnp.concatenate([small, jnp.zeros((PAD, PAD), jnp.float32)], axis=1) + unit
    for k in range(rank):
        row = both[k:k + 1, :]
        pivot = both[k:k + 1, k:k + 1]
        column = both[:, k:k + 1] * (1.0 / pivot)
        both = both - jnp.where(rows > k, column, 0.0) * row
    diagonal = jnp.sum(jnp.where(lanes == rows, both, 0.0), axis=1, keepdims=True)
    inside = lax.broadcasted_iota(jnp.int32, (PAD, 1), 0) < rank
    scale = jnp.where(inside, lax.rsqrt(jnp.where(inside, diagonal, 1.0)), 0.0)
    return both[:, PAD:] * scale


def subspace_kernel(rank, gram_ref, start_ref, out_ref):
    g1, g2, g3 = split(gram_ref[...])
    basis = start_ref[...]
    for _ in range(ITERS):
        b1, b2, b3 = split(basis)
        by1 = matmul(jnp.concatenate([b1, b2, b3], axis=0), g1)
        by2 = matmul(jnp.concatenate([b1, b2], axis=0), g2)
        by3 = matmul(b1, g3)
        z = (by3 + by1[2 * PAD:] + by2[PAD:]) + (by1[PAD:2 * PAD] + by2[:PAD]) + by1[:PAD]
        z1, z2, z3 = split(z)
        s = matmul_t(jnp.concatenate([z1, z2, z3], axis=0), jnp.concatenate([z1, z2, z3], axis=0))
        small = (s[:PAD, 2 * PAD:] + s[2 * PAD:, :PAD] + s[PAD:2 * PAD, PAD:2 * PAD]) + (s[:PAD, PAD:2 * PAD] + s[PAD:2 * PAD, :PAD]) + s[:PAD, :PAD]
        w1, w2, w3 = split(inverse_factor(small, rank))
        basis = (matmul(w3, z1) + matmul(w1, z3) + matmul(w2, z2)) + (matmul(w2, z1) + matmul(w1, z2)) + matmul(w1, z1)
    out_ref[...] = basis


def subspace(gram, start):
    width, rank = start.shape
    start_t = jnp.pad(start.T, ((0, PAD - rank), (0, 0)))
    return pl.pallas_call(
        functools.partial(subspace_kernel, rank),
        out_shape=jax.ShapeDtypeStruct((PAD, width), jnp.float32),
        in_specs=[pl.BlockSpec(memory_space=pltpu.VMEM)] * 2,
        out_specs=pl.BlockSpec(memory_space=pltpu.VMEM),
        compiler_params=pltpu.CompilerParams(vmem_limit_bytes=32 * 1024 * 1024),
    )(gram, start_t)


def partner(value, axis, size, bits):
    return lax.ppermute(value, axis, [(i, i ^ bits) for i in range(size)])


def spread(block, axis, size):
    return lax.all_to_all(jnp.broadcast_to(block, (size,) + block.shape), axis, 0, 0)


def per_device(field, start_x, start_y):
    rows_y, rows_z, count_var, width_x = field.shape
    rank = start_x.shape[1]
    size_y, size_z = lax.axis_size("gy"), lax.axis_size("gz")
    flat = field.reshape(rows_y * rows_z * count_var, width_x)
    columns = flat.shape[0] * size_y * size_z
    partial = product(flat.T, flat).reshape(size_y, width_x // size_y, width_x)
    block = jnp.sum(lax.all_to_all(partial, "gy", 0, 0), axis=0)
    p = [block] + [partner(block, "gz", size_z, bits) for bits in range(1, 8)]
    block = ((p[0] + p[1]) + (p[2] + p[3])) + ((p[4] + p[5]) + (p[6] + p[7]))
    p = [block] + [partner(block, "gz", size_z, bits) for bits in (8, 16, 24)]
    block = ((p[0] + p[1]) + (p[2] + p[3])) / columns
    gram_x = spread(block, "gy", size_y).reshape(width_x, width_x)
    factor_x = subspace(gram_x, start_x)[:rank].T
    reduced = product(flat, factor_x).reshape(rows_y, rows_z * count_var * rank)
    columns_y = rows_z * count_var * rank * size_z
    total_y = rows_y * size_y
    whole = spread(reduced, "gy", size_y).reshape(total_y, -1)
    block = product(reduced, whole.T)
    for bits in (1, 2, 4, 8, 16):
        block = block + partner(block, "gz", size_z, bits)
    gram_y = spread(block / columns_y, "gy", size_y).reshape(total_y, total_y)
    factor_t = subspace(gram_y, start_y)[:rank]
    core = product(factor_t, whole)
    first_row = lax.axis_index("gy") * rows_y
    factor_y = lax.dynamic_slice_in_dim(factor_t.T, first_row, rows_y, 0)
    core = core / jnp.sqrt(jnp.float32(width_x * total_y))
    return (factor_x, factor_y, core.reshape(rank, rows_z, count_var * rank))


def solution(mesh):
    placed = (P("gy", "gz", None, None), P(), P())
    return jax.shard_map(
        per_device,
        mesh=mesh,
        in_specs=placed,
        out_specs=(P(), P("gy", None), P(None, "gz", None)),
        check_vma=False,
    )
```

```python
import functools

import jax
import jax.numpy as jnp
from jax import lax
from jax.experimental import pallas as pl
from jax.experimental.pallas import tpu as pltpu
from jax.sharding import PartitionSpec as P

ITERS = 4
PAD = 64
LANES = 128
PANEL = 4
PLANE = ("gy", "core")
VMEM = pl.BlockSpec(memory_space=pltpu.VMEM)
LIMIT = pltpu.CompilerParams(vmem_limit_bytes=48 * 1024 * 1024)


def split2(value):
    high = value.astype(jnp.bfloat16)
    return high, (value - high.astype(jnp.float32)).astype(jnp.bfloat16)


def split3(value):
    high = value.astype(jnp.bfloat16)
    rest = value - high.astype(jnp.float32)
    middle = rest.astype(jnp.bfloat16)
    return high, middle, (rest - middle.astype(jnp.float32)).astype(jnp.bfloat16)


def dot(left, right, dims):
    return lax.dot_general(left, right, ((dims[:1], dims[1:]), ((), ())), preferred_element_type=jnp.float32)


def upper_blocks(count):
    return [(i, j) for i in range(count) for j in range(i, count)]


def unpack(packed_ref, width):
    count = width // LANES
    blocks = {
        pair: packed_ref[LANES * n:LANES * (n + 1), :] for n, pair in enumerate(upper_blocks(count))
    }
    rows = [
        jnp.concatenate([blocks[(i, j)] if i <= j else blocks[(j, i)].T for j in range(count)], axis=1)
        for i in range(count)
    ]
    return jnp.concatenate(rows, axis=0)


def unit_trace(gram):
    eye = lax.broadcasted_iota(jnp.int32, gram.shape, 0) == lax.broadcasted_iota(jnp.int32, gram.shape, 1)
    diagonal = jnp.sum(jnp.where(eye, gram, 0.0), axis=0, keepdims=True)
    return gram * (1.0 / jnp.sum(diagonal, axis=1, keepdims=True))


def inverse_factor(small, rank):
    iota = functools.partial(lax.broadcasted_iota, jnp.int32)
    rows, lanes = iota((PAD, 2 * PAD), 0), iota((PAD, 2 * PAD), 1)
    both = jnp.concatenate([small, jnp.zeros((PAD, PAD), jnp.float32)], axis=1)
    both = both + jnp.where(lanes == rows + PAD, 1.0, 0.0)
    tiles = [both[8 * t:8 * t + 8, :] for t in range(PAD // 8)]
    within = iota((8, LANES), 0)
    for start in range(0, rank, PANEL):
        first = start // 8
        cols = [
            {t: jnp.broadcast_to(tiles[t][:, start + j:start + j + 1], (8, LANES)) for t in range(first, PAD // 8)}
            for j in range(PANEL)
        ]
        base = start - 8 * first
        lines = [jnp.broadcast_to(tiles[first][base + j:base + j + 1, :], (8, LANES)) for j in range(PANEL)]
        factors = []
        for j in range(PANEL):
            def at(column, row):
                return jnp.broadcast_to(column[first][base + row:base + row + 1, :], (8, LANES))
            inverse = 1.0 / at(cols[j], j)
            factor = {t: column * inverse for t, column in cols[j].items()}
            ahead = [at(cols[n], j) for n in range(j + 1, PANEL)]
            factor[first] = jnp.where(within > base + j, factor[first], 0.0)
            for n in range(j + 1, PANEL):
                lines[n] = lines[n] - at(factor, n) * lines[j]
                cols[n] = {t: column - factor[t] * ahead[n - j - 1] for t, column in cols[n].items()}
            factors.append(factor)
        for t in range(first, PAD // 8):
            change = factors[0][t] * lines[0]
            for j in range(1, PANEL):
                change = change + factors[j][t] * lines[j]
            tiles[t] = tiles[t] - change
    both = jnp.concatenate(tiles, axis=0)
    diagonal = jnp.sum(jnp.where(lanes == rows, both, 0.0), axis=1, keepdims=True)
    inside = iota((PAD, 1), 0) < rank
    scale = jnp.where(inside, lax.rsqrt(jnp.where(inside, diagonal, 1.0)), 0.0)
    return both[:, PAD:] * scale


def subspace(gram, basis, rank):
    g1, g2, g3 = split3(gram)
    for step in range(ITERS):
        b1, b2, b3 = split3(basis)
        by1 = dot(jnp.concatenate([b1, b2, b3], axis=0), g1, (1, 0))
        by2 = dot(jnp.concatenate([b1, b2], axis=0), g2, (1, 0))
        by3 = dot(b1, g3, (1, 0))
        z = (by3 + by1[2 * PAD:] + by2[PAD:]) + (by1[PAD:2 * PAD] + by2[:PAD]) + by1[:PAD]
        basis = z
        if step % 2 == 0:
            continue
        z1, z2, z3 = split3(z)
        zs = jnp.concatenate([z1, z2, z3], axis=0)
        s = dot(zs, zs, (1, 1))
        small = (s[:PAD, 2 * PAD:] + s[2 * PAD:, :PAD] + s[PAD:2 * PAD, PAD:2 * PAD]) + (s[:PAD, PAD:2 * PAD] + s[PAD:2 * PAD, :PAD]) + s[:PAD, :PAD]
        w1, w2, w3 = split3(inverse_factor(small, rank))
        left = jnp.concatenate([w1, w1, w2, w2, w1, w3], axis=1)
        right = jnp.concatenate([z1, z2, z1, z2, z3, z1], axis=0)
        basis = dot(left, right, (1, 0))
    return basis


def padded(start_ref):
    rank, width = start_ref.shape
    return jnp.concatenate([start_ref[...], jnp.zeros((PAD - rank, width), jnp.float32)], axis=0)


def gram_kernel(dims, field_ref, packed_ref, high_ref, middle_ref):
    count_y, count_v, count_z, tiles_x = dims
    stride = count_v * tiles_x * count_z
    rows = []
    for z in range(count_z):
        for v in range(count_v):
            rows.append(jnp.concatenate(
                [field_ref[pl.ds((v * tiles_x + t) * count_z + z, count_y, stride=stride), :] for t in range(tiles_x)], axis=1))
    high, middle = split2(jnp.concatenate(rows, axis=0))
    high_ref[...] = high
    middle_ref[...] = middle
    done = 0
    for i in range(tiles_x // 2):
        part = slice(2 * LANES * i, 2 * LANES * (i + 1))
        rest = slice(2 * LANES * i, None)
        gram = dot(high[:, part], middle[:, rest], (0, 0)) + dot(middle[:, part], high[:, rest], (0, 0))
        gram = gram + dot(high[:, part], high[:, rest], (0, 0))
        for half in range(2):
            for j in range(half, gram.shape[1] // LANES):
                packed_ref[done:done + LANES, :] = gram[LANES * half:LANES * (half + 1), LANES * j:LANES * (j + 1)]
                done += LANES


def x_kernel(packed_ref, start_ref, high_ref, middle_ref, factor_ref, chunks_ref, pairs_ref):
    rank, width = start_ref.shape
    devices, count_y, _ = chunks_ref.shape
    basis = subspace(unit_trace(unpack(packed_ref, width)), padded(start_ref), rank)
    factor_ref[...] = basis[:rank]
    f1, f2 = split2(basis)
    high, middle = high_ref[...], middle_ref[...]
    reduced = (dot(high, f2, (1, 1)) + dot(middle, f1, (1, 1))) + dot(high, f1, (1, 1))
    count = reduced.shape[0] // count_y
    blocks = [reduced[count_y * n:count_y * (n + 1), :] for n in range(count)]
    blank = jnp.zeros((count_y, PAD), jnp.float32)
    per = chunks_ref.shape[2] // PAD
    for d in range(devices):
        parts = [blocks[n] if n < count else blank for n in range(per * d, per * (d + 1))]
        chunks_ref[d] = jnp.concatenate(parts, axis=1)
    for n in range(count // 2):
        pairs_ref[count_y * n:count_y * (n + 1), :] = jnp.concatenate(blocks[2 * n:2 * n + 2], axis=1)


def y_gram_kernel(columns_ref, gram_ref):
    a1, a2 = split2(columns_ref[...])
    gram = (dot(a1, a2, (1, 1)) + dot(a2, a1, (1, 1))) + dot(a1, a1, (1, 1))
    width = gram.shape[0]
    for n in range(width // LANES):
        gram_ref[width * n:width * (n + 1), :] = gram[:, LANES * n:LANES * (n + 1)]


def y_kernel(gram_ref, start_ref, factor_ref):
    rank, width = start_ref.shape
    gram = jnp.concatenate([gram_ref[width * n:width * (n + 1), :] for n in range(width // LANES)], axis=1)
    factor_ref[...] = subspace(unit_trace(gram), padded(start_ref), rank)


def core_kernel(dims, scale, factor_ref, whole_ref, out_ref):
    rank, count_z, count_v, count_y = dims
    devices = whole_ref.shape[0]
    f1, f2 = split2(factor_ref[...])
    columns = [
        jnp.concatenate([whole_ref[d, count_y * n:count_y * (n + 1), :] for d in range(devices)], axis=0)
        for n in range(count_z * count_v // 2)
    ]
    a1, a2 = split2(jnp.concatenate(columns, axis=1))
    core = ((dot(f1, a2, (1, 0)) + dot(f2, a1, (1, 0))) + dot(f1, a1, (1, 0))) * scale
    for z in range(count_z):
        out_ref[z] = jnp.concatenate(
            [core[:rank, PAD * n:PAD * n + rank] for n in range(z * count_v, (z + 1) * count_v)], axis=1)


def call(kernel, shapes, *args):
    return pl.pallas_call(
        kernel,
        out_shape=shapes,
        in_specs=[VMEM] * len(args),
        out_specs=jax.tree.map(lambda _: VMEM, shapes),
        compiler_params=LIMIT,
    )(*args)


def shape(dims, kind=jnp.float32):
    return jax.ShapeDtypeStruct(dims, kind)


def spread(block, axes):
    copies = jnp.broadcast_to(block, (lax.axis_size(axes),) + block.shape)
    return lax.all_to_all(copies, axes, 0, 0)


def total(packed, factor):
    size = lax.axis_size(PLANE)
    parts = packed.reshape(size, packed.shape[0] // size, LANES)
    block = jnp.sum(lax.all_to_all(parts, PLANE, 0, 0), axis=0)
    block = jnp.sum(spread(block, "z"), axis=0) * factor
    return spread(block, PLANE).reshape(packed.shape)


def per_device(field, start_x, start_y):
    rows_y, rows_z, count_var, width_x = field.shape
    rank = start_x.shape[1]
    size_y, size_z = lax.axis_size("gy"), lax.axis_size(("z", "core"))
    total_y = rows_y * size_y
    tiles_x = width_x // LANES
    count = rows_z * count_var
    view = field.transpose(0, 2, 1, 3).reshape(rows_y * count_var, rows_z, tiles_x, LANES)
    view = view.transpose(0, 2, 1, 3).reshape(-1, LANES)
    blocks_x = len(upper_blocks(tiles_x))
    flat = (rows_y * count, width_x)
    packed, high, middle = call(
        functools.partial(gram_kernel, (rows_y, count_var, rows_z, tiles_x)),
        (shape((blocks_x * LANES, LANES)), shape(flat, jnp.bfloat16), shape(flat, jnp.bfloat16)),
        view)
    packed = total(packed, 1.0 / (flat[0] * size_y * size_z))
    per = -(-count // size_y)
    factor_x, chunks, pairs = call(
        x_kernel,
        (shape((rank, width_x)), shape((size_y, rows_y, per * PAD)), shape((flat[0] // 2, 2 * PAD))),
        packed, start_x.T, high, middle)
    whole = lax.all_gather(pairs, "gy")
    columns = lax.all_to_all(chunks, "gy", 0, 0).reshape(total_y, per * PAD)
    gram_y = call(y_gram_kernel, shape((total_y * (total_y // LANES), LANES)), columns)
    gram_y = total(gram_y, 1.0 / (count * rank * size_z))
    factor_t = call(y_kernel, shape((PAD, total_y)), gram_y, start_y.T)
    mine = lax.dynamic_slice_in_dim(factor_t, lax.axis_index("gy") * rows_y, rows_y, 1)
    core = call(
        functools.partial(core_kernel, (rank, rows_z, count_var, rows_y), 1.0 / float(width_x * total_y) ** 0.5),
        shape((rows_z, rank, count_var * rank)),
        factor_t, whole)
    return (factor_x.T, mine[:rank].T, core.transpose(1, 0, 2))


def solution(mesh):
    size_y, size_z = mesh.devices.shape
    inner = jax.sharding.Mesh(mesh.devices.reshape(size_y, size_z // 2, 2), ("gy", "z", "core"))
    along_z = ("z", "core")
    return jax.shard_map(
        per_device,
        mesh=inner,
        in_specs=(P("gy", along_z, None, None), P(), P()),
        out_specs=(P(), P("gy", None), P(None, along_z, None)),
        check_vma=False,
    )
```
